128 devices in a mesh: dip: 64 (over y, z, x_hi, core), rep: 2 (over x_lo).
Axes of the slice: x: 4 (x_hi: 2, x_lo: 2; x = x_hi * 2 + x_lo), y: 4, z: 4, core: 2. Of those that a mesh axis runs over, the one named last changes fastest.
Arguments:
- slip_field: float32 [4096, 8192], P('dip', 'rep'), may hold values from -4 to 4
- state_field: float32 [4096, 8192], P('dip', 'rep'), may hold values from 0.5 to 2
- direct_effect: float32 [4096, 8192], P('dip', 'rep'), may hold values from 1 to 2
- load_stress: float32 [4096, 8192], P('dip', 'rep'), may hold values from -1 to 1
- kernel_spectrum: float32 [8192, 8192], P(('dip', 'rep')), may hold values from -0.5 to 0.5
Outputs:
- velocity: float32 [4096, 8192], P('dip', 'rep')
- state_next: float32 [4096, 8192], P('dip', 'rep')
The draws below stay inside these ranges and needn't reach their ends.
All inputs are finite; a program needn't handle non-finite values.
Results may differ from the reference program's by a relative error of at most 0.00005.
Values sent between devices are 32-bit elements; how exact they have to be, the bound alone decides.
A program may use at most 128 MiB of HBM per device.

```python
import math
import jax
import jax.numpy as jnp

ND = 4096
NS = 8192


def draw_slip_field(key, part):
    key = jax.random.fold_in(key, 11)
    return jnp.clip(jax.random.normal(key, (ND, NS), jnp.float32), -4.0, 4.0)


def block_levels(own_key, dims, pieces, low, largest):
    gain = 1.0
    for dim, shards_of in pieces:
        steps = jax.random.uniform(jax.random.fold_in(jax.random.fold_in(own_key, 6), dim), (shards_of,), jnp.float32, low / len(pieces), largest / len(pieces))
        gain = gain * jnp.repeat(jnp.exp(steps), dims[dim] // shards_of).reshape((-1,) + (1,) * (len(dims) - 1 - dim))
    return gain


def setup_inputs(seed: int = 0) -> dict:
    key_list = jax.random.split(jax.random.key(seed), 6)
    return {
        "slip_field": draw_slip_field(jax.random.fold_in(key_list[5], 71), 0),
        "state_field": jnp.clip(jnp.exp(math.log(2.0) - 1.3862944 * jax.random.uniform(key_list[1], (ND, NS), jnp.float32) ** block_levels(key_list[1], (ND, NS), ((0, 64), (1, 2)), -0.2, 0.2)), 0.5, 2.0),
        "direct_effect": jnp.clip(jnp.exp(math.log(2.0) - 0.6931472 * jax.random.uniform(key_list[2], (ND, NS), jnp.float32) ** block_levels(key_list[2], (ND, NS), ((0, 64), (1, 2)), -0.2, 0.2)), 1.0, 2.0),
        "load_stress": jnp.clip(jax.random.uniform(key_list[3], (ND, NS), jnp.float32, -1.0, 1.0) * block_levels(key_list[3], (ND, NS), ((0, 64), (1, 2)), -0.4, 0.0), -1.0, 1.0),
        "kernel_spectrum": jnp.clip(jax.random.uniform(key_list[4], (NS, 2 * ND), jnp.float32, -0.5, 0.5) * block_levels(key_list[4], (NS, 2 * ND), ((0, 128),), -0.4, 0.0), -0.5, 0.5),
    }


time_step = 0.5
state_exponent = 0.8


def reference(slip_field, state_field, direct_effect, load_stress, kernel_spectrum):
    fault_rows = slip_field.shape[0]
    mirrored = jnp.concatenate([slip_field, slip_field[::-1]], axis=0)
    spectrum = jnp.fft.fft2(mirrored)
    product = spectrum * kernel_spectrum.T
    elastic = jnp.real(jnp.fft.ifft2(product))[:fault_rows].astype(jnp.float32)
    stress = load_stress + elastic
    velocity = 2.0 * jnp.sinh(stress / direct_effect) * jnp.exp(-state_exponent * jnp.log(state_field) / direct_effect)
    state_next = (state_field + time_step) / (1.0 + time_step * jnp.abs(velocity))
    return velocity, state_next
```

```python
import functools

import jax
import jax.numpy as jnp
from jax import lax
from jax.experimental import pallas as pl
from jax.experimental.pallas import tpu as pltpu
from jax.sharding import PartitionSpec as P

MESH = pl.DeviceIdType.MESH

time_step = 0.5
state_exponent = 0.8
full_turn = 6.283185307179586
highest = lax.Precision.HIGHEST


def phases(index, period, sign):
    angle = sign * full_turn / period * (index % period).astype(jnp.float32)
    return (jnp.cos(angle), jnp.sin(angle))


def index_grid(first, second):
    return (
        lax.broadcasted_iota(jnp.int32, (first, second), 0),
        lax.broadcasted_iota(jnp.int32, (first, second), 1),
    )


def contract(form, real_part, imag_part, table):
    cos_part, sin_part = table
    out_real = jnp.einsum(form, real_part, cos_part, precision=highest) - jnp.einsum(
        form, imag_part, sin_part, precision=highest
    )
    out_imag = jnp.einsum(form, real_part, sin_part, precision=highest) + jnp.einsum(
        form, imag_part, cos_part, precision=highest
    )
    return (out_real, out_imag)


def twiddle(real_part, imag_part, table):
    cos_part, sin_part = table
    return (
        real_part * cos_part - imag_part * sin_part,
        real_part * sin_part + imag_part * cos_part,
    )


def exchange_body(count, rows, src_ref, dst_ref, own_sem, send_sem, recv_sem):
    me = lax.axis_index("dip") * 2 + lax.axis_index("rep")
    barrier = pltpu.get_barrier_semaphore()

    def partner(step):
        mixed = lax.rem(step * 37, count - 1)
        return jnp.bitwise_xor(me, jnp.where(mixed == 0, count - 1, mixed))

    def greet(step, carry):
        other = partner(step)
        pl.semaphore_signal(
            barrier, inc=1, device_id=(other // 2, other % 2), device_id_type=MESH
        )
        return carry

    lax.fori_loop(1, count, greet, 0)
    own = pltpu.make_async_copy(
        src_ref.at[pl.ds(me * rows, rows)], dst_ref.at[pl.ds(me * rows, rows)], own_sem
    )
    own.start()
    pl.semaphore_wait(barrier, count - 1)

    def send(step, carry):
        other = partner(step)
        pltpu.make_async_remote_copy(
            src_ref=src_ref.at[pl.ds(other * rows, rows)],
            dst_ref=dst_ref.at[pl.ds(me * rows, rows)],
            send_sem=send_sem,
            recv_sem=recv_sem,
            device_id=(other // 2, other % 2),
            device_id_type=MESH,
        ).start()
        return carry

    lax.fori_loop(1, count, send, 0)
    rest = pltpu.make_async_remote_copy(
        src_ref=src_ref.at[pl.ds(0, (count - 1) * rows)],
        dst_ref=dst_ref.at[pl.ds(0, (count - 1) * rows)],
        send_sem=send_sem,
        recv_sem=recv_sem,
        device_id=(0, 0),
        device_id_type=MESH,
    )
    rest.wait_recv()
    rest.wait_send()
    own.wait()


def exchange(packets, collective_id):
    count = packets.shape[0]
    flat = packets.reshape(-1, 128)
    rows = flat.shape[0] // count
    return pl.pallas_call(
        functools.partial(exchange_body, count, rows),
        out_shape=jax.ShapeDtypeStruct(flat.shape, flat.dtype),
        in_specs=[pl.BlockSpec(memory_space=pltpu.VMEM)],
        out_specs=pl.BlockSpec(memory_space=pltpu.VMEM),
        scratch_shapes=[pltpu.SemaphoreType.DMA(())] * 3,
        compiler_params=pltpu.CompilerParams(
            collective_id=collective_id, has_side_effects=True, vmem_limit_bytes=16 * 2**20
        ),
    )(flat)


def shards(slip_field, state_field, direct_effect, load_stress, kernel_spectrum):
    dip_count = lax.axis_size("dip")
    rep_count = lax.axis_size("rep")
    dev_rows = slip_field.shape[0]
    dev_cols = slip_field.shape[1]
    strike_len = dev_cols * rep_count
    groups = dip_count * rep_count
    block_freq = strike_len // groups
    sub_rows = dev_rows // rep_count
    dip_blocks = 2 * dip_count
    dip_len = dip_blocks * dev_rows
    halves = slip_field[None]
    image_count = halves.shape[0]
    lines = lax.all_to_all(halves, "rep", split_axis=1, concat_axis=2, tiled=True)
    lanes = lines.reshape(image_count, sub_rows, groups, block_freq)
    outer_idx, freq_idx = index_grid(groups, groups)
    first_table = phases(outer_idx * freq_idx, groups, -1.0)
    spec_real = jnp.einsum("hkba,bq->hkaq", lanes, first_table[0], precision=highest)
    spec_imag = jnp.einsum("hkba,bq->hkaq", lanes, first_table[1], precision=highest)
    inner_idx, freq_idx = index_grid(block_freq, groups)
    spec_real, spec_imag = twiddle(
        spec_real, spec_imag, phases(inner_idx * freq_idx, strike_len, -1.0)
    )
    inner_idx, high_idx = index_grid(block_freq, block_freq)
    spec_real, spec_imag = contract(
        "hkaq,ar->rqhk", spec_real, spec_imag, phases(inner_idx * high_idx, block_freq, -1.0)
    )
    packet = jnp.stack([spec_real, spec_imag], axis=2)
    received = exchange(packet.reshape(groups, -1), 1)
    received = received.reshape(
        dip_count, rep_count, block_freq, 2, image_count, sub_rows
    ).transpose(2, 0, 1, 3, 4, 5)
    received = jnp.concatenate([received, received[:, ::-1, ::-1, :, :, ::-1]], axis=4)
    image_count = received.shape[4]
    part_real = received[:, :, :, 0]
    part_imag = received[:, :, :, 1]
    dev_idx = lax.broadcasted_iota(jnp.int32, (dip_count, image_count, dip_blocks), 0)
    half_idx = lax.broadcasted_iota(jnp.int32, (dip_count, image_count, dip_blocks), 1)
    out_idx = lax.broadcasted_iota(jnp.int32, (dip_count, image_count, dip_blocks), 2)
    dip_table = phases((dev_idx + dip_count * half_idx) * out_idx, dip_blocks, -1.0)
    wave_real, wave_imag = contract("fprhk,phq->frkq", part_real, part_imag, dip_table)
    wave_real = wave_real.reshape(block_freq, dev_rows, dip_blocks)
    wave_imag = wave_imag.reshape(block_freq, dev_rows, dip_blocks)
    row_idx, out_grid = index_grid(dev_rows, dip_blocks)
    wave_real, wave_imag = twiddle(wave_real, wave_imag, phases(row_idx * out_grid, dip_len, -1.0))
    row_idx, high_idx = index_grid(dev_rows, dev_rows)
    wave_real, wave_imag = contract(
        "faq,ar->frq", wave_real, wave_imag, phases(row_idx * high_idx, dev_rows, -1.0)
    )
    wave_real = wave_real.reshape(block_freq, dip_len)
    wave_imag = wave_imag.reshape(block_freq, dip_len)
    prod_real = (kernel_spectrum * wave_real).reshape(block_freq, dev_rows, dip_blocks)
    prod_imag = (kernel_spectrum * wave_imag).reshape(block_freq, dev_rows, dip_blocks)
    high_idx, row_idx = index_grid(dev_rows, dev_rows)
    back_real, back_imag = contract(
        "fqb,qa->fab", prod_real, prod_imag, phases(high_idx * row_idx, dev_rows, 1.0)
    )
    row_idx, out_grid = index_grid(dev_rows, dip_blocks)
    back_real, back_imag = twiddle(back_real, back_imag, phases(row_idx * out_grid, dip_len, 1.0))
    out_grid, dev_grid = index_grid(dip_blocks, dip_count)
    back_real, back_imag = contract(
        "fab,bp->paf", back_real, back_imag, phases(out_grid * dev_grid, dip_blocks, 1.0)
    )
    scale_inv = 1.0 / dip_len
    stacked = (
        jnp.stack(
            [
                back_real.reshape(dip_count, rep_count, sub_rows, block_freq),
                back_imag.reshape(dip_count, rep_count, sub_rows, block_freq),
            ],
            axis=2,
        )
        * scale_inv
    )
    returned = exchange(stacked.reshape(groups, -1), 2)
    returned = returned.reshape(groups, 2, sub_rows, block_freq)
    block_idx, outer_idx = index_grid(groups, groups)
    line_real, line_imag = contract(
        "ekf,ea->kaf", returned[:, 0], returned[:, 1], phases(block_idx * outer_idx, groups, 1.0)
    )
    outer_idx, inner_idx = index_grid(groups, block_freq)
    line_real, line_imag = twiddle(
        line_real, line_imag, phases(outer_idx * inner_idx, strike_len, 1.0)
    )
    inner_idx, low_idx = index_grid(block_freq, block_freq)
    last_cos, last_sin = phases(inner_idx * low_idx, block_freq, 1.0)
    elastic = jnp.einsum("kaf,fb->kba", line_real, last_cos, precision=highest) - jnp.einsum(
        "kaf,fb->kba", line_imag, last_sin, precision=highest
    )
    elastic = elastic.reshape(sub_rows, strike_len) * (1.0 / strike_len)
    elastic = lax.all_to_all(elastic, "rep", split_axis=1, concat_axis=0, tiled=True)
    stress = load_stress + elastic
    velocity = (
        2.0
        * jnp.sinh(stress / direct_effect)
        * jnp.exp(-state_exponent * jnp.log(state_field) / direct_effect)
    )
    state_next = (state_field + time_step) / (1.0 + time_step * jnp.abs(velocity))
    return (velocity, state_next)


def solution(mesh):
    placed = (
        P("dip", "rep"),
        P("dip", "rep"),
        P("dip", "rep"),
        P("dip", "rep"),
        P(("dip", "rep"), None),
    )
    return jax.shard_map(
        shards,
        mesh=mesh,
        in_specs=placed,
        out_specs=(P("dip", "rep"), P("dip", "rep")),
        check_vma=False,
    )
```

```python
import functools

import jax
import jax.numpy as jnp
import ml_dtypes
import numpy as np
from jax import lax
from jax.experimental import pallas as pl
from jax.experimental.pallas import tpu as pltpu
from jax.sharding import PartitionSpec as P

MESH = pl.DeviceIdType.MESH
F32 = jnp.float32
BF16 = jnp.bfloat16

time_step = 0.5
state_exponent = 0.8

ND = 4096
NS = 8192
COUNT = 128
LINES = 32
SLOTS = 32
CHUNKS = 2
QUADS = SLOTS // 4 // CHUNKS
ROWS = 2 * QUADS


def wave(product, period):
    angle = 2.0 * np.pi * (np.asarray(product, np.float64) / period)
    return np.cos(angle), np.sin(angle)


def halves(table):
    high = table.astype(ml_dtypes.bfloat16)
    low = (table - high.astype(np.float64)).astype(ml_dtypes.bfloat16)
    return high, low


def tables():
    out = {}
    f32 = np.float32
    v0 = np.arange(64)
    n1 = np.arange(64)
    n0 = np.arange(128)
    cos, sin = wave(np.outer(v0, n1), 64)
    high, low = halves(np.concatenate([cos, -sin], 0))
    out["t1"] = np.concatenate([high, high, low], 1)
    cos, sin = wave(np.outer(v0, n0), 8192)
    out["tw1c"], out["tw1s"] = cos.astype(f32), sin.astype(f32)
    for name, v1 in (("t2a", np.arange(64)), ("t2b", np.arange(63, -1, -1))):
        cos, sin = wave(np.outer(v1, n0), 128)
        full = np.concatenate(
            [np.concatenate([cos, sin], 1), np.concatenate([-sin, cos], 1)], 0
        )
        out[name] = np.concatenate(halves(full), 0)
        back = np.concatenate(
            [np.concatenate([cos, sin], 1), np.concatenate([-sin, cos], 1)], 0
        )
        high, low = halves(back)
        out[name.replace("t2", "t7")] = np.concatenate([high, high, low], 0)
    alt = np.zeros((64, 128))
    alt[0] = 1.0 - 2.0 * (n0 % 2)
    out["alt"] = alt.astype(ml_dtypes.bfloat16)
    s = np.arange(128)
    u0 = np.arange(256)
    u1 = np.arange(16)
    k = np.arange(32) + 0.5
    cos, sin = wave(np.outer(u0, s), 256)
    high, low = halves(np.concatenate([cos, -sin], 0))
    out["t3"] = np.concatenate([high, high, low], 1)
    cos, sin = wave(np.outer(u0, k), 8192)
    out["tw3c"], out["tw3s"] = np.tile(cos, (1, 4)).astype(f32), np.tile(sin, (1, 4)).astype(f32)
    cos, sin = wave(np.outer(u1, k), 32)
    eye = np.eye(4)
    full = np.concatenate([np.kron(eye, cos), np.kron(eye, sin)], 1)
    out["t4"] = np.concatenate(halves(full), 0)
    cos, sin = np.kron(eye, cos.T), np.kron(eye, sin.T)
    full = np.concatenate([np.concatenate([cos, -sin], 1), np.concatenate([sin, cos], 1)], 0)
    high, low = halves(full)
    out["t5"] = np.concatenate([high, high, low], 1)
    cos, sin = wave(np.outer(k, u0), 8192)
    out["tw5c"], out["tw5s"] = np.tile(cos, (4, 1)).astype(f32), np.tile(sin, (4, 1)).astype(f32)
    cos, sin = wave(np.outer(s, u0), 256)
    out["t6"] = np.concatenate(halves(np.concatenate([cos, -sin], 1)), 0)
    flip = np.zeros((256, 256))
    flip[(256 - u0) % 256, u0] = 1.0
    out["flip"] = flip.astype(ml_dtypes.bfloat16)
    cos, sin = wave(np.outer(n1, v0), 64)
    high, low = halves(np.concatenate([cos, -sin], 1))
    out["t8"] = np.concatenate([high, high, low], 1)
    return out


def split(value):
    high = value.astype(BF16)
    low = (value - high.astype(F32)).astype(BF16)
    return high, low


def dot(a, b):
    return lax.dot_general(a, b, (((1,), (0,)), ((), ())), preferred_element_type=F32)


def dot_t(a, b):
    return lax.dot_general(a, b, (((1,), (1,)), ((), ())), preferred_element_type=F32)


def table_dot(table, value):
    high, low = split(value)
    return dot(table, jnp.concatenate([high, low, high], 0))


def table_dot_t(table, value):
    high, low = split(value)
    rows = table.shape[0] // 2
    both = dot_t(table, high)
    return both[:rows] + both[rows:] + dot_t(table[:rows], low)


NAMES = (
    ("t1", "tw1c", "tw1s", "t2a", "t2b", "t7a", "t7b", "alt", "t8")
    + ("t3", "tw3c", "tw3s", "t4", "t5", "tw5c", "tw5s", "t6", "flip")
)


def body(slip, spectrum, *refs):
    count = len(NAMES)
    elastic = refs[count]
    tab = dict(zip(NAMES, refs[count + 1 : 2 * count + 1]))
    staged = {
        name: pltpu.make_async_copy(refs[i], tab[name], refs[2 * count + 1].at[i])
        for i, name in enumerate(NAMES)
    }
    (
        xin, xr, yr, yi, snd, rcv, pos, neg, edge,
        pd, pr, nd, nr, a_re, a_im, b_all, snd2, rcv2, ebuf, xout, sems, chunk_sems, out_sems,
    ) = refs[2 * count + 2 :]
    rep = lax.axis_index("rep")
    me = lax.axis_index("dip") * 2 + rep
    barrier = pltpu.get_barrier_semaphore()

    def place(other):
        return (other // 2, other % 2)

    def partner(step):
        mixed = lax.rem(step * 37, COUNT - 1)
        return jnp.bitwise_xor(me, jnp.where(mixed == 0, COUNT - 1, mixed))

    def greet(step, carry):
        pl.semaphore_signal(
            barrier, inc=1, device_id=place(partner(step)), device_id_type=MESH
        )
        return carry

    lax.fori_loop(1, COUNT, greet, 0)

    for name in NAMES:
        staged[name].start()
    own_slip = pltpu.make_async_copy(slip.at[pl.ds(rep * LINES, LINES)], xin.at[rep], sems.at[0])
    own_slip.start()
    low_side = me < COUNT // 2
    own_k_pos = pltpu.make_async_copy(spectrum.at[pl.ds(0, SLOTS)], pos, sems.at[1])
    own_k_neg = pltpu.make_async_copy(spectrum.at[pl.ds(0, SLOTS)], neg, sems.at[1])
    own_edge = pltpu.make_async_copy(spectrum.at[pl.ds(SLOTS, 1)], edge, sems.at[2])

    @pl.when(low_side)
    def _():
        own_k_pos.start()

    @pl.when(jnp.logical_not(low_side))
    def _():
        own_k_neg.start()
        own_edge.start()

    pl.semaphore_wait(barrier, COUNT - 1)

    near = place(jnp.bitwise_xor(me, 1))
    slip_out = pltpu.make_async_remote_copy(
        src_ref=slip.at[pl.ds((1 - rep) * LINES, LINES)],
        dst_ref=xin.at[rep],
        send_sem=sems.at[3],
        recv_sem=sems.at[4],
        device_id=near,
        device_id_type=MESH,
    )
    slip_out.start()

    mirror = place(COUNT - 1 - me)
    upper = spectrum.at[pl.ds(SLOTS, SLOTS)]
    k_to_pos = pltpu.make_async_remote_copy(
        src_ref=upper, dst_ref=pos, send_sem=sems.at[5], recv_sem=sems.at[6],
        device_id=mirror, device_id_type=MESH,
    )
    k_to_neg = pltpu.make_async_remote_copy(
        src_ref=upper, dst_ref=neg, send_sem=sems.at[5], recv_sem=sems.at[6],
        device_id=mirror, device_id_type=MESH,
    )
    edge_target = jnp.where(me == COUNT // 2, 0, COUNT - me)
    edge_out = pltpu.make_async_remote_copy(
        src_ref=spectrum.at[pl.ds(0, 1)], dst_ref=edge, send_sem=sems.at[7],
        recv_sem=sems.at[8], device_id=place(edge_target), device_id_type=MESH,
    )

    @pl.when(low_side)
    def _():
        k_to_pos.start()

    @pl.when(jnp.logical_not(low_side))
    def _():
        k_to_neg.start()
        edge_out.start()

    own_slip.wait()
    slip_out.wait_recv()

    def relay(col, carry):
        for side in range(2):
            lanes = pl.ds(pl.multiple_of(col * 128, 128), 128)
            xr[pl.ds(side * 32 + col, LINES, stride=64), :] = xin[side, :, lanes]
        return carry

    lax.fori_loop(0, 32, relay, 0, unroll=4)
    for name in NAMES:
        staged[name].wait()

    def strike(pair, carry):
        both = jnp.concatenate(
            [xr[pl.ds((2 * pair + i) * 64, 64), :] for i in range(2)], 1
        )
        out = table_dot(tab["t1"][...], both)
        cos, sin = tab["tw1c"][...], tab["tw1s"][...]
        for i in range(2):
            real = out[:64, i * 128 : (i + 1) * 128]
            imag = out[64:, i * 128 : (i + 1) * 128]
            yr[pl.ds(2 * pair + i, 64, stride=LINES), :] = real * cos + imag * sin
            yi[pl.ds(2 * pair + i, 64, stride=LINES), :] = imag * cos - real * sin
        return carry

    lax.fori_loop(0, LINES // 2, strike, 0, unroll=4)

    def exchange(src, dst, chunk, first_sem):
        mine = pl.ds(pl.multiple_of(me * ROWS, ROWS), ROWS)
        own_sem, send_sem, recv_sem = (chunk_sems.at[first_sem + i, chunk] for i in range(3))
        own = pltpu.make_async_copy(src.at[chunk, mine], dst.at[chunk, mine], own_sem)
        own.start()

        def send(step, carry):
            other = partner(step)
            pltpu.make_async_remote_copy(
                src_ref=src.at[chunk, pl.ds(pl.multiple_of(other * ROWS, ROWS), ROWS)],
                dst_ref=dst.at[chunk, mine],
                send_sem=send_sem,
                recv_sem=recv_sem,
                device_id=place(other),
                device_id_type=MESH,
            ).start()
            return carry

        lax.fori_loop(1, COUNT, send, 0)
        rest = pltpu.make_async_remote_copy(
            src_ref=src.at[chunk, pl.ds(0, (COUNT - 1) * ROWS)],
            dst_ref=dst.at[chunk, pl.ds(0, (COUNT - 1) * ROWS)],
            send_sem=send_sem,
            recv_sem=recv_sem,
            device_id=near,
            device_id_type=MESH,
        )
        return own, rest

    def second_stage(chunk, side, quad):
        first = (side * 32 + (chunk * QUADS + quad) * 4) * LINES
        rows = pl.ds(first, 256)
        out = table_dot_t(
            tab["t2b" if side else "t2a"][...], jnp.concatenate([yr[rows, :], yi[rows, :]], 1)
        )
        real, imag = out[:64], out[64:]
        if first == 0:
            high, low = split(yr[pl.ds(0, 128), :])
            alt = tab["alt"][...]
            extra = dot_t(alt, high) + dot_t(alt, low)
            lane = lax.broadcasted_iota(jnp.int32, (64, 128), 1)
            extra = jnp.where(lane < LINES, extra, 0.0)
            imag = jnp.concatenate([imag[:, :128] + extra, imag[:, 128:]], 1)
        for i in range(2):
            cols = slice(i * 128, (i + 1) * 128)
            start = side * 64 * ROWS + quad + i
            snd[chunk, pl.ds(start, 64, stride=ROWS), :] = real[:, cols]
            snd[chunk, pl.ds(start + QUADS, 64, stride=ROWS), :] = imag[:, cols]

    forward = []
    for chunk in range(CHUNKS):
        for side in range(2):
            for quad in range(0, QUADS, 2):
                second_stage(chunk, side, quad)
        forward.append(exchange(snd, rcv, chunk, 0))

    @pl.when(low_side)
    def _():
        own_k_pos.wait()
        k_to_neg.wait_recv()
        edge_out.wait_recv()

    @pl.when(jnp.logical_not(low_side))
    def _():
        own_k_neg.wait()
        own_edge.wait()
        k_to_pos.wait_recv()

    def fold(source, direct, back, rows, first):
        lane = lax.broadcasted_iota(jnp.int32, (rows, 128), 1)

        def load(tile):
            lanes = pl.ds(pl.multiple_of(tile * 128, 128), 128)
            return source[:, lanes] if rows < 8 else source[pl.ds(first, rows), lanes]

        base = first * 16 if rows >= 8 else SLOTS * 16

        def step(block, carry):
            for half in range(2):
                stride = dict(stride=16) if rows > 1 else {}
                direct[half, pl.ds(base + block, rows, **stride), :] = load(2 * block + half)
                value = load(32 + 2 * block + half)
                if half == 0:
                    after = load(jnp.minimum(32 + 2 * block + 2, 62))
                    after = jnp.where(block == 15, 0.0, after)
                    value = jnp.where(lane == 0, after, value)
                back[half, pl.ds(base + 15 - block, rows, **stride), :] = value
            return carry

        lax.fori_loop(0, 16, step, 0)

    fold(pos, pd, pr, SLOTS, 0)
    fold(neg, nd, nr, SLOTS, 0)
    fold(edge, nd, nr, 1, 0)

    def flip(back, rows):
        high, low = split(jnp.concatenate([back[0, rows, :], back[1, rows, :]], 1))
        return dot(high, tab["flip"][...]) + dot(low, tab["flip"][...])

    scale = 2.0 / (float(NS) * float(2 * ND))

    def combine(slot, carry):
        rows = pl.ds(pl.multiple_of(slot * 16, 16), 16)
        other = pl.ds(pl.multiple_of((SLOTS - slot) * 16, 16), 16)
        plus = jnp.concatenate([pd[0, rows, :], pd[1, rows, :]], 1)
        minus = jnp.concatenate([nd[0, other, :], nd[1, other, :]], 1)
        plus_back = flip(pr, rows)
        minus_back = flip(nr, other)
        packed = jnp.logical_and(me == 0, slot == 0)
        even_plus = (plus + plus_back) * scale
        even_minus = (minus + minus_back) * scale
        odd = ((plus - plus_back) - (minus - minus_back)) * scale
        both = even_plus + even_minus
        a_re[rows, :] = jnp.where(packed, even_plus, both)
        a_im[rows, :] = jnp.where(packed, even_minus, both)
        b_all[rows, :] = jnp.where(packed, 0.0, odd)
        return carry

    lax.fori_loop(0, SLOTS, combine, 0, unroll=4)

    def dip(chunk, quad, carry):
        got = jnp.concatenate(
            [rcv[chunk, pl.ds(comp * QUADS + quad, COUNT, stride=ROWS), :] for comp in range(2)], 1
        )
        first = table_dot(tab["t3"][...], got)
        cos, sin = tab["tw3c"][...], tab["tw3s"][...]
        spec = []
        for comp in range(2):
            real = first[:256, comp * 128 : (comp + 1) * 128]
            imag = first[256:, comp * 128 : (comp + 1) * 128]
            turned = jnp.concatenate([real * cos + imag * sin, imag * cos - real * sin], 1)
            spec.append(table_dot_t(tab["t4"][...], turned))
        rows = pl.ds(pl.multiple_of((chunk * QUADS + quad) * 64, 64), 64)
        b = b_all[rows, :]
        cos, sin = tab["tw5c"][...], tab["tw5s"][...]
        turned = []
        for even, odd in (
            (spec[0] * a_re[rows, :], spec[1] * b),
            (spec[1] * a_im[rows, :], -spec[0] * b),
        ):
            out = table_dot(tab["t5"][...], jnp.concatenate([even, odd], 0))
            real, imag = out[:128], out[128:]
            turned.append(
                jnp.concatenate([real * cos - imag * sin, real * sin + imag * cos], 1)
            )
        out = table_dot_t(tab["t6"][...], jnp.concatenate(turned, 0))
        for comp in range(2):
            snd2[chunk, pl.ds(comp * QUADS + quad, COUNT, stride=ROWS), :] = out[
                :, comp * 128 : (comp + 1) * 128
            ]
        return carry

    backward = []
    for chunk in range(CHUNKS):
        own, rest = forward[chunk]
        own.wait()
        rest.wait_recv()
        lax.fori_loop(0, QUADS, functools.partial(dip, chunk), 0, unroll=4)
        backward.append(exchange(snd2, rcv2, chunk, 3))

    def unstrike(chunk, side, quad, carry):
        start = side * 64 * ROWS + quad
        got = jnp.concatenate(
            [
                rcv2[chunk, pl.ds(start + comp * QUADS, 64, stride=ROWS), :]
                for comp in range(2)
            ],
            0,
        )
        high, low = split(got.T)
        out = dot(jnp.concatenate([high, low, high], 1), tab["t7b" if side else "t7a"][...])
        real, imag = out[:, :128], out[:, 128:]
        if side == 0 and chunk == 0:
            alt = tab["alt"][...]
            extra = dot(high[:, 64:], alt) + dot(low[:, 64:], alt)
            line = lax.broadcasted_iota(jnp.int32, (128, 128), 0)
            keep = jnp.logical_and(line < LINES, quad == 0)
            real = real + jnp.where(keep, extra, 0.0)
        for part in range(4):
            freq = side * 32 + (chunk * QUADS + quad) * 4 + part
            cos = tab["tw1c"][pl.ds(freq, 1), :]
            sin = tab["tw1s"][pl.ds(freq, 1), :]
            rows = pl.ds(pl.multiple_of(freq * LINES, LINES), LINES)
            r, i = real[part * 32 : part * 32 + 32], imag[part * 32 : part * 32 + 32]
            yr[rows, :] = r * cos - i * sin
            yi[rows, :] = r * sin + i * cos
        return carry

    for chunk in range(CHUNKS):
        own, rest = backward[chunk]
        own.wait()
        rest.wait_recv()
        for side in range(2):
            lax.fori_loop(
                0, QUADS, functools.partial(unstrike, chunk, side), 0, unroll=4
            )

    def last(pair, carry):
        both = jnp.concatenate(
            [
                jnp.concatenate(
                    [
                        yr[pl.ds(2 * pair + i, 64, stride=LINES), :],
                        yi[pl.ds(2 * pair + i, 64, stride=LINES), :],
                    ],
                    0,
                )
                for i in range(2)
            ],
            1,
        )
        out = table_dot(tab["t8"][...], both)
        for i in range(2):
            ebuf[pl.ds(2 * pair + i, 64, stride=LINES), :] = out[:, i * 128 : (i + 1) * 128]
        return carry

    def relay_back(first, side, dst, dst_first, col, carry):
        rows = pl.ds(pl.multiple_of((side * 32 + col) * LINES + first, 8), 8)
        lanes = pl.ds(pl.multiple_of(col * 128, 128), 128)
        dst[pl.ds(pl.multiple_of(dst_first, 8), 8), lanes] = ebuf[rows, :]
        return carry

    outgoing = []
    for part in range(LINES // 8):
        first = part * 8
        lax.fori_loop(part * 4, part * 4 + 4, last, 0, unroll=4)
        away = functools.partial(relay_back, first, 1 - rep, xout, first)
        lax.fori_loop(0, 32, away, 0, unroll=8)
        copy = pltpu.make_async_remote_copy(
            src_ref=xout.at[pl.ds(first, 8)],
            dst_ref=elastic.at[pl.ds(pl.multiple_of(rep * LINES + first, 8), 8)],
            send_sem=out_sems.at[0, part],
            recv_sem=out_sems.at[1, part],
            device_id=near,
            device_id_type=MESH,
        )
        copy.start()
        outgoing.append(copy)
    for part in range(LINES // 8):
        home = functools.partial(
            relay_back, part * 8, rep, elastic, rep * LINES + part * 8
        )
        lax.fori_loop(0, 32, home, 0, unroll=8)

    slip_out.wait_send()
    for own, rest in forward + backward:
        rest.wait_send()

    @pl.when(low_side)
    def _():
        k_to_pos.wait_send()

    @pl.when(jnp.logical_not(low_side))
    def _():
        k_to_neg.wait_send()
        edge_out.wait_send()

    for copy in outgoing:
        copy.wait()


def elastic_stress(slip_field, kernel_spectrum):
    made = tables()
    arrays = [jnp.asarray(made[name]) for name in NAMES]
    vmem = pl.BlockSpec(memory_space=pltpu.VMEM)
    flat = (64 * LINES, 128)
    packets = (CHUNKS, COUNT * ROWS, 128)
    return pl.pallas_call(
        body,
        out_shape=jax.ShapeDtypeStruct((64, 4096), F32),
        in_specs=[pl.BlockSpec(memory_space=pl.ANY)] * (2 + len(arrays)),
        out_specs=vmem,
        scratch_shapes=[pltpu.VMEM(a.shape, a.dtype) for a in arrays]
        + [pltpu.SemaphoreType.DMA((len(arrays),))]
        + [
            pltpu.VMEM((2, LINES, 4096), F32),
            pltpu.VMEM(flat, F32),
            pltpu.VMEM(flat, F32),
            pltpu.VMEM(flat, F32),
            pltpu.VMEM(packets, F32),
            pltpu.VMEM(packets, F32),
            pltpu.VMEM((SLOTS, 8192), F32),
            pltpu.VMEM((SLOTS, 8192), F32),
            pltpu.VMEM((1, 8192), F32),
            pltpu.VMEM((2, 512, 128), F32),
            pltpu.VMEM((2, 512, 128), F32),
            pltpu.VMEM((2, 528, 128), F32),
            pltpu.VMEM((2, 528, 128), F32),
            pltpu.VMEM((512, 256), F32),
            pltpu.VMEM((512, 256), F32),
            pltpu.VMEM((512, 256), F32),
            pltpu.VMEM(packets, F32),
            pltpu.VMEM(packets, F32),
            pltpu.VMEM(flat, F32),
            pltpu.VMEM((LINES, 4096), F32),
            pltpu.SemaphoreType.DMA((9,)),
            pltpu.SemaphoreType.DMA((6, CHUNKS)),
            pltpu.SemaphoreType.DMA((2, LINES // 8)),
        ],
        compiler_params=pltpu.CompilerParams(
            collective_id=1, has_side_effects=True, vmem_limit_bytes=60 * 2**20
        ),
        name="elastic_stress",
    )(slip_field, kernel_spectrum, *arrays)


def shards(slip_field, state_field, direct_effect, load_stress, kernel_spectrum):
    elastic = elastic_stress(slip_field, kernel_spectrum)
    stress = load_stress + elastic
    velocity = (
        2.0
        * jnp.sinh(stress / direct_effect)
        * jnp.exp(-state_exponent * jnp.log(state_field) / direct_effect)
    )
    state_next = (state_field + time_step) / (1.0 + time_step * jnp.abs(velocity))
    return (velocity, state_next)


def solution(mesh):
    placed = (
        P("dip", "rep"),
        P("dip", "rep"),
        P("dip", "rep"),
        P("dip", "rep"),
        P(("dip", "rep"), None),
    )
    return jax.shard_map(
        shards,
        mesh=mesh,
        in_specs=placed,
        out_specs=(P("dip", "rep"), P("dip", "rep")),
        check_vma=False,
    )
```

```python
import functools

import jax
import jax.numpy as jnp
import ml_dtypes
import numpy as np
from jax import lax
from jax.experimental import pallas as pl
from jax.experimental.pallas import tpu as pltpu
from jax.sharding import PartitionSpec as P

MESH = pl.DeviceIdType.MESH
F32 = jnp.float32
BF16 = jnp.bfloat16

time_step = 0.5
state_exponent = 0.8

ND = 4096
NS = 8192
COUNT = 128
LINES = 32
SLOTS = 32
CHUNKS = 4
EARLY = 2
QUADS = SLOTS // 4 // CHUNKS
ROWS = 2 * QUADS


def wave(product, period):
    angle = 2.0 * np.pi * (np.asarray(product, np.float64) / period)
    return np.cos(angle), np.sin(angle)


def halves(table):
    high = table.astype(ml_dtypes.bfloat16)
    low = (table - high.astype(np.float64)).astype(ml_dtypes.bfloat16)
    return high, low


def tables():
    out = {}
    f32 = np.float32
    v0 = np.arange(64)
    n1 = np.arange(64)
    n0 = np.arange(128)
    cos, sin = wave(np.outer(v0, n1), 64)
    high, low = halves(np.concatenate([cos, -sin], 0))
    out["t1"] = np.concatenate([high, high, low], 1)
    cos, sin = wave(np.outer(v0, n0), 8192)
    out["tw1c"], out["tw1s"] = cos.astype(f32), sin.astype(f32)
    for name, v1 in (("t2a", np.arange(64)), ("t2b", np.arange(63, -1, -1))):
        cos, sin = wave(np.outer(v1, n0), 128)
        full = np.concatenate(
            [np.concatenate([cos, sin], 1), np.concatenate([-sin, cos], 1)], 0
        )
        out[name] = np.concatenate(halves(full), 0)
        back = np.concatenate(
            [np.concatenate([cos, sin], 1), np.concatenate([-sin, cos], 1)], 0
        )
        high, low = halves(back)
        out[name.replace("t2", "t7")] = np.concatenate([high, high, low], 0)
    alt = np.zeros((64, 128))
    alt[0] = 1.0 - 2.0 * (n0 % 2)
    out["alt"] = alt.astype(ml_dtypes.bfloat16)
    s = np.arange(128)
    u0 = np.arange(256)
    u1 = np.arange(16)
    k = np.arange(32) + 0.5
    cos, sin = wave(np.outer(u0, s), 256)
    high, low = halves(np.concatenate([cos, -sin], 0))
    out["t3"] = np.concatenate([high, high, low], 1)
    cos, sin = wave(np.outer(u0, k), 8192)
    out["tw3c"], out["tw3s"] = np.tile(cos, (1, 4)).astype(f32), np.tile(sin, (1, 4)).astype(f32)
    cos, sin = wave(np.outer(u1, k), 32)
    eye = np.eye(4)
    full = np.concatenate([np.kron(eye, cos), np.kron(eye, sin)], 1)
    out["t4"] = np.concatenate(halves(full), 0)
    cos, sin = np.kron(eye, cos.T), np.kron(eye, sin.T)
    full = np.concatenate([np.concatenate([cos, -sin], 1), np.concatenate([sin, cos], 1)], 0)
    high, low = halves(full)
    out["t5"] = np.concatenate([high, high, low], 1)
    cos, sin = wave(np.outer(k, u0), 8192)
    out["tw5c"], out["tw5s"] = np.tile(cos, (4, 1)).astype(f32), np.tile(sin, (4, 1)).astype(f32)
    cos, sin = wave(np.outer(s, u0), 256)
    out["t6"] = np.concatenate(halves(np.concatenate([cos, -sin], 1)), 0)
    flip = np.zeros((256, 256))
    flip[(256 - u0) % 256, u0] = 1.0
    out["flip"] = flip.astype(ml_dtypes.bfloat16)
    cos, sin = wave(np.outer(n1, v0), 64)
    high, low = halves(np.concatenate([cos, -sin], 1))
    out["t8"] = np.concatenate([high, high, low], 1)
    return out


def split(value):
    high = value.astype(BF16)
    low = (value - high.astype(F32)).astype(BF16)
    return high, low


def dot(a, b):
    return lax.dot_general(a, b, (((1,), (0,)), ((), ())), preferred_element_type=F32)


def dot_t(a, b):
    return lax.dot_general(a, b, (((1,), (1,)), ((), ())), preferred_element_type=F32)


def table_dot(table, value):
    high, low = split(value)
    return dot(table, jnp.concatenate([high, low, high], 0))


def table_dot_t(table, value):
    high, low = split(value)
    rows = table.shape[0] // 2
    both = dot_t(table, high)
    return both[:rows] + both[rows:] + dot_t(table[:rows], low)


NAMES = (
    ("t1", "tw1c", "tw1s", "t2a", "t2b", "t7a", "t7b", "alt", "t8")
    + ("t3", "tw3c", "tw3s", "t4", "t5", "tw5c", "tw5s", "t6", "flip")
)


def body(slip, spectrum, *refs):
    count = len(NAMES)
    elastic = refs[count]
    tab = dict(zip(NAMES, refs[count + 1 : 2 * count + 1]))
    staged = {
        name: pltpu.make_async_copy(refs[i], tab[name], refs[2 * count + 1].at[i])
        for i, name in enumerate(NAMES)
    }
    (
        xin, xr, yr, yi, snd, rcv, pos, neg, edge,
        pd, pr, nd, nr, a_re, a_im, b_all, snd2, rcv2, ebuf, xout, sems, k_sems, chunk_sems, out_sems,
    ) = refs[2 * count + 2 :]
    rep = lax.axis_index("rep")
    me = lax.axis_index("dip") * 2 + rep
    barrier = pltpu.get_barrier_semaphore()

    def place(other):
        return (lax.shift_right_logical(other, 1), jnp.bitwise_and(other, 1))

    def partner(step):
        return jnp.bitwise_xor(me, jnp.bitwise_and(step * 37, COUNT - 1))

    def greet(step, carry):
        pl.semaphore_signal(
            barrier, inc=1, device_id=place(partner(step)), device_id_type=MESH
        )
        return carry

    lax.fori_loop(1, COUNT, greet, 0)

    for name in NAMES:
        staged[name].start()
    own_slip = pltpu.make_async_copy(slip.at[pl.ds(rep * LINES, LINES)], xin.at[rep], sems.at[0])
    own_slip.start()
    low_side = me < COUNT // 2
    own_k_pos = pltpu.make_async_copy(spectrum.at[pl.ds(0, SLOTS)], pos, sems.at[1])
    own_k_neg = pltpu.make_async_copy(spectrum.at[pl.ds(0, SLOTS)], neg, sems.at[1])
    own_edge = pltpu.make_async_copy(spectrum.at[pl.ds(SLOTS, 1)], edge, sems.at[2])

    @pl.when(low_side)
    def _():
        own_k_pos.start()

    @pl.when(jnp.logical_not(low_side))
    def _():
        own_k_neg.start()
        own_edge.start()

    pl.semaphore_wait(barrier, COUNT - 1)

    near = place(jnp.bitwise_xor(me, 1))
    slip_out = pltpu.make_async_remote_copy(
        src_ref=slip.at[pl.ds((1 - rep) * LINES, LINES)],
        dst_ref=xin.at[rep],
        send_sem=sems.at[3],
        recv_sem=sems.at[4],
        device_id=near,
        device_id_type=MESH,
    )
    slip_out.start()

    mirror = place(COUNT - 1 - me)
    part_rows = SLOTS // CHUNKS

    def kernel_rows(chunk, dst, first):
        return pltpu.make_async_remote_copy(
            src_ref=spectrum.at[pl.ds(SLOTS + first, part_rows)],
            dst_ref=dst.at[pl.ds(first, part_rows)],
            send_sem=k_sems.at[0, chunk],
            recv_sem=k_sems.at[1, chunk],
            device_id=mirror,
            device_id_type=MESH,
        )

    k_to_pos = [kernel_rows(c, pos, c * part_rows) for c in range(CHUNKS)]
    k_to_neg = [kernel_rows(c, neg, SLOTS - (c + 1) * part_rows) for c in range(CHUNKS)]
    edge_target = jnp.where(me == COUNT // 2, 0, COUNT - me)
    edge_out = pltpu.make_async_remote_copy(
        src_ref=spectrum.at[pl.ds(0, 1)], dst_ref=edge, send_sem=sems.at[7],
        recv_sem=sems.at[8], device_id=place(edge_target), device_id_type=MESH,
    )

    def send_kernel_rows(first, stop):
        @pl.when(low_side)
        def _():
            for copy in k_to_pos[first:stop]:
                copy.start()

        @pl.when(jnp.logical_not(low_side))
        def _():
            if first == 0:
                edge_out.start()
            for copy in k_to_neg[first:stop]:
                copy.start()

    send_kernel_rows(0, EARLY)

    own_slip.wait()
    slip_out.wait_recv()

    def relay(col, carry):
        for side in range(2):
            lanes = pl.ds(pl.multiple_of(col * 128, 128), 128)
            xr[pl.ds(side * 32 + col, LINES, stride=64), :] = xin[side, :, lanes]
        return carry

    lax.fori_loop(0, 32, relay, 0, unroll=4)
    for name in NAMES:
        staged[name].wait()

    def strike(pair, carry):
        both = jnp.concatenate(
            [xr[pl.ds((2 * pair + i) * 64, 64), :] for i in range(2)], 1
        )
        out = table_dot(tab["t1"][...], both)
        cos, sin = tab["tw1c"][...], tab["tw1s"][...]
        for i in range(2):
            real = out[:64, i * 128 : (i + 1) * 128]
            imag = out[64:, i * 128 : (i + 1) * 128]
            yr[pl.ds(2 * pair + i, 64, stride=LINES), :] = real * cos + imag * sin
            yi[pl.ds(2 * pair + i, 64, stride=LINES), :] = imag * cos - real * sin
        return carry

    lax.fori_loop(0, LINES // 2, strike, 0, unroll=4)

    def exchange(src, dst, chunk, first_sem):
        mine = pl.ds(pl.multiple_of(me * ROWS, ROWS), ROWS)
        own_sem, send_sem, recv_sem = (chunk_sems.at[first_sem + i, chunk] for i in range(3))
        own = pltpu.make_async_copy(src.at[chunk, mine], dst.at[chunk, mine], own_sem)
        own.start()

        def send(step, carry):
            other = partner(step)
            pltpu.make_async_remote_copy(
                src_ref=src.at[chunk, pl.ds(pl.multiple_of(other * ROWS, ROWS), ROWS)],
                dst_ref=dst.at[chunk, mine],
                send_sem=send_sem,
                recv_sem=recv_sem,
                device_id=place(other),
                device_id_type=MESH,
            ).start()
            return carry

        lax.fori_loop(1, COUNT, send, 0)
        rest = pltpu.make_async_remote_copy(
            src_ref=src.at[chunk, pl.ds(0, (COUNT - 1) * ROWS)],
            dst_ref=dst.at[chunk, pl.ds(0, (COUNT - 1) * ROWS)],
            send_sem=send_sem,
            recv_sem=recv_sem,
            device_id=near,
            device_id_type=MESH,
        )
        return own, rest

    def second_stage(chunk, side, quad):
        first = (side * 32 + (chunk * QUADS + quad) * 4) * LINES
        rows = pl.ds(first, 256)
        out = table_dot_t(
            tab["t2b" if side else "t2a"][...], jnp.concatenate([yr[rows, :], yi[rows, :]], 1)
        )
        real, imag = out[:64], out[64:]
        if first == 0:
            high, low = split(yr[pl.ds(0, 128), :])
            alt = tab["alt"][...]
            extra = dot_t(alt, high) + dot_t(alt, low)
            lane = lax.broadcasted_iota(jnp.int32, (64, 128), 1)
            extra = jnp.where(lane < LINES, extra, 0.0)
            imag = jnp.concatenate([imag[:, :128] + extra, imag[:, 128:]], 1)
        for i in range(2):
            cols = slice(i * 128, (i + 1) * 128)
            start = side * 64 * ROWS + quad + i
            snd[chunk, pl.ds(start, 64, stride=ROWS), :] = real[:, cols]
            snd[chunk, pl.ds(start + QUADS, 64, stride=ROWS), :] = imag[:, cols]

    forward = []
    for chunk in range(CHUNKS):
        for side in range(2):
            for quad in range(0, QUADS, 2):
                second_stage(chunk, side, quad)
        forward.append(exchange(snd, rcv, chunk, 0))
    send_kernel_rows(EARLY, CHUNKS)

    @pl.when(low_side)
    def _():
        own_k_pos.wait()
        edge_out.wait_recv()

    @pl.when(jnp.logical_not(low_side))
    def _():
        own_k_neg.wait()
        own_edge.wait()

    def fold(source, direct, back, rows, first):
        lane = lax.broadcasted_iota(jnp.int32, (rows, 128), 1)

        def load(tile):
            lanes = pl.ds(pl.multiple_of(tile * 128, 128), 128)
            return source[:, lanes] if rows < 8 else source[pl.ds(first, rows), lanes]

        base = first * 16 if rows >= 8 else SLOTS * 16

        def step(block, carry):
            for half in range(2):
                stride = dict(stride=16) if rows > 1 else {}
                direct[half, pl.ds(base + block, rows, **stride), :] = load(2 * block + half)
                value = load(32 + 2 * block + half)
                if half == 0:
                    after = load(jnp.minimum(32 + 2 * block + 2, 62))
                    after = jnp.where(block == 15, 0.0, after)
                    value = jnp.where(lane == 0, after, value)
                back[half, pl.ds(base + 15 - block, rows, **stride), :] = value
            return carry

        lax.fori_loop(0, 16, step, 0, unroll=4)

    fold(edge, nd, nr, 1, 0)

    def flip(back, rows):
        high, low = split(jnp.concatenate([back[0, rows, :], back[1, rows, :]], 1))
        return dot(high, tab["flip"][...]) + dot(low, tab["flip"][...])

    scale = 2.0 / (float(NS) * float(2 * ND))

    def combine(slot, carry):
        rows = pl.ds(pl.multiple_of(slot * 16, 16), 16)
        other = pl.ds(pl.multiple_of((SLOTS - slot) * 16, 16), 16)
        plus = jnp.concatenate([pd[0, rows, :], pd[1, rows, :]], 1)
        minus = jnp.concatenate([nd[0, other, :], nd[1, other, :]], 1)
        plus_back = flip(pr, rows)
        minus_back = flip(nr, other)
        packed = jnp.logical_and(me == 0, slot == 0)
        even_plus = (plus + plus_back) * scale
        even_minus = (minus + minus_back) * scale
        odd = ((plus - plus_back) - (minus - minus_back)) * scale
        both = even_plus + even_minus
        a_re[rows, :] = jnp.where(packed, even_plus, both)
        a_im[rows, :] = jnp.where(packed, even_minus, both)
        b_all[rows, :] = jnp.where(packed, 0.0, odd)
        return carry

    def prepare(chunk):
        @pl.when(low_side)
        def _():
            k_to_neg[chunk].wait_recv()

        @pl.when(jnp.logical_not(low_side))
        def _():
            k_to_pos[chunk].wait_recv()

        fold(pos, pd, pr, part_rows, chunk * part_rows)
        fold(neg, nd, nr, part_rows, SLOTS - (chunk + 1) * part_rows)
        first = chunk * part_rows
        lax.fori_loop(first, first + part_rows, combine, 0, unroll=4)

    def dip(chunk, quad, carry):
        got = jnp.concatenate(
            [rcv[chunk, pl.ds(comp * QUADS + quad, COUNT, stride=ROWS), :] for comp in range(2)], 1
        )
        first = table_dot(tab["t3"][...], got)
        cos, sin = tab["tw3c"][...], tab["tw3s"][...]
        spec = []
        for comp in range(2):
            real = first[:256, comp * 128 : (comp + 1) * 128]
            imag = first[256:, comp * 128 : (comp + 1) * 128]
            turned = jnp.concatenate([real * cos + imag * sin, imag * cos - real * sin], 1)
            spec.append(table_dot_t(tab["t4"][...], turned))
        rows = pl.ds(pl.multiple_of((chunk * QUADS + quad) * 64, 64), 64)
        b = b_all[rows, :]
        cos, sin = tab["tw5c"][...], tab["tw5s"][...]
        turned = []
        for even, odd in (
            (spec[0] * a_re[rows, :], spec[1] * b),
            (spec[1] * a_im[rows, :], -spec[0] * b),
        ):
            out = table_dot(tab["t5"][...], jnp.concatenate([even, odd], 0))
            real, imag = out[:128], out[128:]
            turned.append(
                jnp.concatenate([real * cos - imag * sin, real * sin + imag * cos], 1)
            )
        out = table_dot_t(tab["t6"][...], jnp.concatenate(turned, 0))
        for comp in range(2):
            snd2[chunk, pl.ds(comp * QUADS + quad, COUNT, stride=ROWS), :] = out[
                :, comp * 128 : (comp + 1) * 128
            ]
        return carry

    backward = []
    for chunk in range(CHUNKS):
        prepare(chunk)
        own, rest = forward[chunk]
        own.wait()
        rest.wait_recv()
        lax.fori_loop(0, QUADS, functools.partial(dip, chunk), 0, unroll=QUADS)
        backward.append(exchange(snd2, rcv2, chunk, 3))

    def unstrike(chunk, side, quad, carry):
        start = side * 64 * ROWS + quad
        got = jnp.concatenate(
            [
                rcv2[chunk, pl.ds(start + comp * QUADS, 64, stride=ROWS), :]
                for comp in range(2)
            ],
            0,
        )
        high, low = split(got.T)
        out = dot(jnp.concatenate([high, low, high], 1), tab["t7b" if side else "t7a"][...])
        real, imag = out[:, :128], out[:, 128:]
        if side == 0 and chunk == 0:
            alt = tab["alt"][...]
            extra = dot(high[:, 64:], alt) + dot(low[:, 64:], alt)
            line = lax.broadcasted_iota(jnp.int32, (128, 128), 0)
            keep = jnp.logical_and(line < LINES, quad == 0)
            real = real + jnp.where(keep, extra, 0.0)
        for part in range(4):
            freq = side * 32 + (chunk * QUADS + quad) * 4 + part
            cos = tab["tw1c"][pl.ds(freq, 1), :]
            sin = tab["tw1s"][pl.ds(freq, 1), :]
            rows = pl.ds(pl.multiple_of(freq * LINES, LINES), LINES)
            r, i = real[part * 32 : part * 32 + 32], imag[part * 32 : part * 32 + 32]
            yr[rows, :] = r * cos - i * sin
            yi[rows, :] = r * sin + i * cos
        return carry

    for chunk in range(CHUNKS):
        own, rest = backward[chunk]
        own.wait()
        rest.wait_recv()
        for side in range(2):
            lax.fori_loop(
                0, QUADS, functools.partial(unstrike, chunk, side), 0, unroll=QUADS
            )

    def last(pair, carry):
        both = jnp.concatenate(
            [
                jnp.concatenate(
                    [
                        yr[pl.ds(2 * pair + i, 64, stride=LINES), :],
                        yi[pl.ds(2 * pair + i, 64, stride=LINES), :],
                    ],
                    0,
                )
                for i in range(2)
            ],
            1,
        )
        out = table_dot(tab["t8"][...], both)
        for i in range(2):
            ebuf[pl.ds(2 * pair + i, 64, stride=LINES), :] = out[:, i * 128 : (i + 1) * 128]
        return carry

    def relay_back(first, side, dst, dst_first, col, carry):
        rows = pl.ds(pl.multiple_of((side * 32 + col) * LINES + first, 8), 8)
        lanes = pl.ds(pl.multiple_of(col * 128, 128), 128)
        dst[pl.ds(pl.multiple_of(dst_first, 8), 8), lanes] = ebuf[rows, :]
        return carry

    outgoing = []
    for part in range(LINES // 8):
        first = part * 8
        lax.fori_loop(part * 4, part * 4 + 4, last, 0, unroll=4)
        away = functools.partial(relay_back, first, 1 - rep, xout, first)
        lax.fori_loop(0, 32, away, 0, unroll=8)
        copy = pltpu.make_async_remote_copy(
            src_ref=xout.at[pl.ds(first, 8)],
            dst_ref=elastic.at[pl.ds(pl.multiple_of(rep * LINES + first, 8), 8)],
            send_sem=out_sems.at[0, part],
            recv_sem=out_sems.at[1, part],
            device_id=near,
            device_id_type=MESH,
        )
        copy.start()
        outgoing.append(copy)
    for part in range(LINES // 8):
        home = functools.partial(
            relay_back, part * 8, rep, elastic, rep * LINES + part * 8
        )
        lax.fori_loop(0, 32, home, 0, unroll=8)

    slip_out.wait_send()
    for own, rest in forward + backward:
        rest.wait_send()

    @pl.when(low_side)
    def _():
        for copy in k_to_pos:
            copy.wait_send()

    @pl.when(jnp.logical_not(low_side))
    def _():
        for copy in k_to_neg:
            copy.wait_send()
        edge_out.wait_send()

    for copy in outgoing:
        copy.wait()


def elastic_stress(slip_field, kernel_spectrum):
    made = tables()
    arrays = [jnp.asarray(made[name]) for name in NAMES]
    vmem = pl.BlockSpec(memory_space=pltpu.VMEM)
    flat = (64 * LINES, 128)
    packets = (CHUNKS, COUNT * ROWS, 128)
    return pl.pallas_call(
        body,
        out_shape=jax.ShapeDtypeStruct((64, 4096), F32),
        in_specs=[pl.BlockSpec(memory_space=pl.ANY)] * (2 + len(arrays)),
        out_specs=vmem,
        scratch_shapes=[pltpu.VMEM(a.shape, a.dtype) for a in arrays]
        + [pltpu.SemaphoreType.DMA((len(arrays),))]
        + [
            pltpu.VMEM((2, LINES, 4096), F32),
            pltpu.VMEM(flat, F32),
            pltpu.VMEM(flat, F32),
            pltpu.VMEM(flat, F32),
            pltpu.VMEM(packets, F32),
            pltpu.VMEM(packets, F32),
            pltpu.VMEM((SLOTS, 8192), F32),
            pltpu.VMEM((SLOTS, 8192), F32),
            pltpu.VMEM((1, 8192), F32),
            pltpu.VMEM((2, 512, 128), F32),
            pltpu.VMEM((2, 512, 128), F32),
            pltpu.VMEM((2, 528, 128), F32),
            pltpu.VMEM((2, 528, 128), F32),
            pltpu.VMEM((512, 256), F32),
            pltpu.VMEM((512, 256), F32),
            pltpu.VMEM((512, 256), F32),
            pltpu.VMEM(packets, F32),
            pltpu.VMEM(packets, F32),
            pltpu.VMEM(flat, F32),
            pltpu.VMEM((LINES, 4096), F32),
            pltpu.SemaphoreType.DMA((9,)),
            pltpu.SemaphoreType.DMA((2, CHUNKS)),
            pltpu.SemaphoreType.DMA((6, CHUNKS)),
            pltpu.SemaphoreType.DMA((2, LINES // 8)),
        ],
        compiler_params=pltpu.CompilerParams(
            collective_id=1, has_side_effects=True, vmem_limit_bytes=60 * 2**20
        ),
        name="elastic_stress",
    )(slip_field, kernel_spectrum, *arrays)


def shards(slip_field, state_field, direct_effect, load_stress, kernel_spectrum):
    elastic = elastic_stress(slip_field, kernel_spectrum)
    stress = load_stress + elastic
    velocity = (
        2.0
        * jnp.sinh(stress / direct_effect)
        * jnp.exp(-state_exponent * jnp.log(state_field) / direct_effect)
    )
    state_next = (state_field + time_step) / (1.0 + time_step * jnp.abs(velocity))
    return (velocity, state_next)


def solution(mesh):
    placed = (
        P("dip", "rep"),
        P("dip", "rep"),
        P("dip", "rep"),
        P("dip", "rep"),
        P(("dip", "rep"), None),
    )
    return jax.shard_map(
        shards,
        mesh=mesh,
        in_specs=placed,
        out_specs=(P("dip", "rep"), P("dip", "rep")),
        check_vma=False,
    )
```

```python
import functools

import jax
import jax.numpy as jnp
import ml_dtypes
import numpy as np
from jax import lax
from jax.experimental import pallas as pl
from jax.experimental.pallas import tpu as pltpu
from jax.sharding import PartitionSpec as P

MESH = pl.DeviceIdType.MESH
F32 = jnp.float32
BF16 = jnp.bfloat16

time_step = 0.5
state_exponent = 0.8

ND = 4096
NS = 8192
COUNT = 128
LINES = 32
SLOTS = 32
CHUNKS = 4
EARLY = 2
QUADS = SLOTS // 4 // CHUNKS
ROWS = 2 * QUADS


def wave(product, period):
    angle = 2.0 * np.pi * (np.asarray(product, np.float64) / period)
    return np.cos(angle), np.sin(angle)


def halves(table):
    high = table.astype(ml_dtypes.bfloat16)
    low = (table - high.astype(np.float64)).astype(ml_dtypes.bfloat16)
    return high, low


def tables():
    out = {}
    f32 = np.float32
    v0 = np.arange(64)
    n1 = np.arange(64)
    n0 = np.arange(128)
    cos, sin = wave(np.outer(v0, n1), 64)
    high, low = halves(np.concatenate([cos, -sin], 0))
    out["t1"] = np.concatenate([high, high, low], 1)
    cos, sin = wave(np.outer(v0, n0), 8192)
    out["tw1c"], out["tw1s"] = cos.astype(f32), sin.astype(f32)
    for name, v1 in (("t2a", np.arange(64)), ("t2b", np.arange(63, -1, -1))):
        cos, sin = wave(np.outer(v1, n0), 128)
        full = np.concatenate(
            [np.concatenate([cos, sin], 1), np.concatenate([-sin, cos], 1)], 0
        )
        out[name] = np.concatenate(halves(full), 0)
        back = np.concatenate(
            [np.concatenate([cos, sin], 1), np.concatenate([-sin, cos], 1)], 0
        )
        high, low = halves(back)
        out[name.replace("t2", "t7")] = np.concatenate([high, high, low], 0)
    alt = np.zeros((64, 128))
    alt[0] = 1.0 - 2.0 * (n0 % 2)
    out["alt"] = alt.astype(ml_dtypes.bfloat16)
    s = np.arange(128)
    u0 = np.arange(256)
    u1 = np.arange(16)
    k = np.arange(32) + 0.5
    cos, sin = wave(np.outer(u0, s), 256)
    high, low = halves(np.concatenate([cos, -sin], 0))
    out["t3"] = np.concatenate([high, high, low], 1)
    cos, sin = wave(np.outer(u0, k), 8192)
    out["tw3c"], out["tw3s"] = np.tile(cos, (1, 4)).astype(f32), np.tile(sin, (1, 4)).astype(f32)
    cos, sin = wave(np.outer(u1, k), 32)
    eye = np.eye(4)
    full = np.concatenate([np.kron(eye, cos), np.kron(eye, sin)], 1)
    out["t4"] = np.concatenate(halves(full), 0)
    cos, sin = np.kron(eye, cos.T), np.kron(eye, sin.T)
    full = np.concatenate([np.concatenate([cos, -sin], 1), np.concatenate([sin, cos], 1)], 0)
    high, low = halves(full)
    out["t5"] = np.concatenate([high, high, low], 1)
    cos, sin = wave(np.outer(k, u0), 8192)
    out["tw5c"], out["tw5s"] = np.tile(cos, (4, 1)).astype(f32), np.tile(sin, (4, 1)).astype(f32)
    cos, sin = wave(np.outer(s, u0), 256)
    out["t6"] = np.concatenate(halves(np.concatenate([cos, -sin], 1)), 0)
    flip = np.zeros((256, 256))
    flip[(256 - u0) % 256, u0] = 1.0
    out["flip"] = flip.astype(ml_dtypes.bfloat16)
    cos, sin = wave(np.outer(n1, v0), 64)
    high, low = halves(np.concatenate([cos, -sin], 1))
    out["t8"] = np.concatenate([high, high, low], 1)
    return out


def split(value):
    high = value.astype(BF16)
    low = (value - high.astype(F32)).astype(BF16)
    return high, low


def dot(a, b):
    return lax.dot_general(a, b, (((1,), (0,)), ((), ())), preferred_element_type=F32)


def dot_t(a, b):
    return lax.dot_general(a, b, (((1,), (1,)), ((), ())), preferred_element_type=F32)


def table_dot(table, value):
    high, low = split(value)
    return dot(table, jnp.concatenate([high, low, high], 0))


def table_dot_t(table, value):
    high, low = split(value)
    rows = table.shape[0] // 2
    both = dot_t(table, high)
    return both[:rows] + both[rows:] + dot_t(table[:rows], low)


NAMES = (
    ("t1", "tw1c", "tw1s", "t2a", "t2b", "t7a", "t7b", "alt", "t8")
    + ("t3", "tw3c", "tw3s", "t4", "t5", "tw5c", "tw5s", "t6", "flip")
)


def body(slip, spectrum, *refs):
    count = len(NAMES)
    elastic = refs[count]
    tab = dict(zip(NAMES, refs[count + 1 : 2 * count + 1]))
    staged = {
        name: pltpu.make_async_copy(refs[i], tab[name], refs[2 * count + 1].at[i])
        for i, name in enumerate(NAMES)
    }
    (
        xin, xr, yr, yi, snd, rcv, pos, neg, edge,
        pd, pr, nd, nr, a_re, a_im, b_all, snd2, rcv2, ebuf, xout, sems, k_sems, chunk_sems, out_sems,
    ) = refs[2 * count + 2 :]
    rep = lax.axis_index("rep")
    me = lax.axis_index("dip") * 2 + rep
    barrier = pltpu.get_barrier_semaphore()

    def place(other):
        return (lax.shift_right_logical(other, 1), jnp.bitwise_and(other, 1))

    def partner(step):
        return jnp.bitwise_xor(me, jnp.bitwise_and(step * 37, COUNT - 1))

    def greet(step, carry):
        pl.semaphore_signal(
            barrier, inc=1, device_id=place(partner(step)), device_id_type=MESH
        )
        return carry

    lax.fori_loop(1, COUNT, greet, 0)

    for name in NAMES:
        staged[name].start()
    own_slip = pltpu.make_async_copy(slip.at[pl.ds(rep * LINES, LINES)], xin.at[rep], sems.at[0])
    own_slip.start()
    low_side = me < COUNT // 2
    own_k_pos = pltpu.make_async_copy(spectrum.at[pl.ds(0, SLOTS)], pos, sems.at[1])
    own_k_neg = pltpu.make_async_copy(spectrum.at[pl.ds(0, SLOTS)], neg, sems.at[1])
    own_edge = pltpu.make_async_copy(spectrum.at[pl.ds(SLOTS, 1)], edge, sems.at[2])

    @pl.when(low_side)
    def _():
        own_k_pos.start()

    @pl.when(jnp.logical_not(low_side))
    def _():
        own_k_neg.start()
        own_edge.start()

    pl.semaphore_wait(barrier, COUNT - 1)

    near = place(jnp.bitwise_xor(me, 1))
    slip_out = pltpu.make_async_remote_copy(
        src_ref=slip.at[pl.ds((1 - rep) * LINES, LINES)],
        dst_ref=xin.at[rep],
        send_sem=sems.at[3],
        recv_sem=sems.at[4],
        device_id=near,
        device_id_type=MESH,
    )
    slip_out.start()

    mirror = place(COUNT - 1 - me)
    part_rows = SLOTS // CHUNKS

    def kernel_rows(chunk, dst, first):
        return pltpu.make_async_remote_copy(
            src_ref=spectrum.at[pl.ds(SLOTS + first, part_rows)],
            dst_ref=dst.at[pl.ds(first, part_rows)],
            send_sem=k_sems.at[0, chunk],
            recv_sem=k_sems.at[1, chunk],
            device_id=mirror,
            device_id_type=MESH,
        )

    k_to_pos = [kernel_rows(c, pos, c * part_rows) for c in range(CHUNKS)]
    k_to_neg = [kernel_rows(c, neg, SLOTS - (c + 1) * part_rows) for c in range(CHUNKS)]
    edge_target = jnp.where(me == COUNT // 2, 0, COUNT - me)
    edge_out = pltpu.make_async_remote_copy(
        src_ref=spectrum.at[pl.ds(0, 1)], dst_ref=edge, send_sem=sems.at[7],
        recv_sem=sems.at[8], device_id=place(edge_target), device_id_type=MESH,
    )

    def send_kernel_rows(first, stop):
        @pl.when(low_side)
        def _():
            for copy in k_to_pos[first:stop]:
                copy.start()

        @pl.when(jnp.logical_not(low_side))
        def _():
            if first == 0:
                edge_out.start()
            for copy in k_to_neg[first:stop]:
                copy.start()

    send_kernel_rows(0, EARLY)

    def fold(source, direct, back, rows, first):
        lane = lax.broadcasted_iota(jnp.int32, (rows, 128), 1)

        def load(tile):
            lanes = pl.ds(pl.multiple_of(tile * 128, 128), 128)
            return source[:, lanes] if rows < 8 else source[pl.ds(first, rows), lanes]

        base = first * 16 if rows >= 8 else SLOTS * 16

        def step(block, carry):
            for half in range(2):
                stride = dict(stride=16) if rows > 1 else {}
                direct[half, pl.ds(base + block, rows, **stride), :] = load(2 * block + half)
                value = load(32 + 2 * block + half)
                if half == 0:
                    after = load(jnp.minimum(32 + 2 * block + 2, 62))
                    after = jnp.where(block == 15, 0.0, after)
                    value = jnp.where(lane == 0, after, value)
                back[half, pl.ds(base + 15 - block, rows, **stride), :] = value
            return carry

        lax.fori_loop(0, 16, step, 0, unroll=4)

    @pl.when(low_side)
    def _():
        own_k_pos.wait()
        fold(pos, pd, pr, SLOTS, 0)

    @pl.when(jnp.logical_not(low_side))
    def _():
        own_k_neg.wait()
        own_edge.wait()
        fold(neg, nd, nr, SLOTS, 0)

    own_slip.wait()
    slip_out.wait_recv()

    def relay(col, carry):
        for side in range(2):
            lanes = pl.ds(pl.multiple_of(col * 128, 128), 128)
            xr[pl.ds(side * 32 + col, LINES, stride=64), :] = xin[side, :, lanes]
        return carry

    lax.fori_loop(0, 32, relay, 0, unroll=4)
    for name in NAMES:
        staged[name].wait()

    def strike(pair, carry):
        both = jnp.concatenate(
            [xr[pl.ds((2 * pair + i) * 64, 64), :] for i in range(2)], 1
        )
        out = table_dot(tab["t1"][...], both)
        cos, sin = tab["tw1c"][...], tab["tw1s"][...]
        for i in range(2):
            real = out[:64, i * 128 : (i + 1) * 128]
            imag = out[64:, i * 128 : (i + 1) * 128]
            yr[pl.ds(2 * pair + i, 64, stride=LINES), :] = real * cos + imag * sin
            yi[pl.ds(2 * pair + i, 64, stride=LINES), :] = imag * cos - real * sin
        return carry

    lax.fori_loop(0, LINES // 2, strike, 0, unroll=4)

    def exchange(src, dst, chunk, first_sem):
        mine = pl.ds(pl.multiple_of(me * ROWS, ROWS), ROWS)
        own_sem, send_sem, recv_sem = (chunk_sems.at[first_sem + i, chunk] for i in range(3))
        own = pltpu.make_async_copy(src.at[chunk, mine], dst.at[chunk, mine], own_sem)
        own.start()

        def send(step, carry):
            other = partner(step)
            pltpu.make_async_remote_copy(
                src_ref=src.at[chunk, pl.ds(pl.multiple_of(other * ROWS, ROWS), ROWS)],
                dst_ref=dst.at[chunk, mine],
                send_sem=send_sem,
                recv_sem=recv_sem,
                device_id=place(other),
                device_id_type=MESH,
            ).start()
            return carry

        lax.fori_loop(1, COUNT, send, 0)
        rest = pltpu.make_async_remote_copy(
            src_ref=src.at[chunk, pl.ds(0, (COUNT - 1) * ROWS)],
            dst_ref=dst.at[chunk, pl.ds(0, (COUNT - 1) * ROWS)],
            send_sem=send_sem,
            recv_sem=recv_sem,
            device_id=near,
            device_id_type=MESH,
        )
        return own, rest

    def second_stage(chunk, side, quad):
        first = (side * 32 + (chunk * QUADS + quad) * 4) * LINES
        rows = pl.ds(first, 256)
        out = table_dot_t(
            tab["t2b" if side else "t2a"][...], jnp.concatenate([yr[rows, :], yi[rows, :]], 1)
        )
        real, imag = out[:64], out[64:]
        if first == 0:
            high, low = split(yr[pl.ds(0, 128), :])
            alt = tab["alt"][...]
            extra = dot_t(alt, high) + dot_t(alt, low)
            lane = lax.broadcasted_iota(jnp.int32, (64, 128), 1)
            extra = jnp.where(lane < LINES, extra, 0.0)
            imag = jnp.concatenate([imag[:, :128] + extra, imag[:, 128:]], 1)
        for i in range(2):
            cols = slice(i * 128, (i + 1) * 128)
            start = side * 64 * ROWS + quad + i
            snd[chunk, pl.ds(start, 64, stride=ROWS), :] = real[:, cols]
            snd[chunk, pl.ds(start + QUADS, 64, stride=ROWS), :] = imag[:, cols]

    forward = []
    for chunk in range(CHUNKS):
        for side in range(2):
            for quad in range(0, QUADS, 2):
                second_stage(chunk, side, quad)
        forward.append(exchange(snd, rcv, chunk, 0))
    send_kernel_rows(EARLY, CHUNKS)

    @pl.when(low_side)
    def _():
        edge_out.wait_recv()

    fold(edge, nd, nr, 1, 0)

    def flip(back, rows):
        high, low = split(jnp.concatenate([back[0, rows, :], back[1, rows, :]], 1))
        return dot(high, tab["flip"][...]) + dot(low, tab["flip"][...])

    scale = 2.0 / (float(NS) * float(2 * ND))

    def combine(slot, carry):
        rows = pl.ds(pl.multiple_of(slot * 16, 16), 16)
        other = pl.ds(pl.multiple_of((SLOTS - slot) * 16, 16), 16)
        plus = jnp.concatenate([pd[0, rows, :], pd[1, rows, :]], 1)
        minus = jnp.concatenate([nd[0, other, :], nd[1, other, :]], 1)
        plus_back = flip(pr, rows)
        minus_back = flip(nr, other)
        packed = jnp.logical_and(me == 0, slot == 0)
        even_plus = (plus + plus_back) * scale
        even_minus = (minus + minus_back) * scale
        odd = ((plus - plus_back) - (minus - minus_back)) * scale
        both = even_plus + even_minus
        a_re[rows, :] = jnp.where(packed, even_plus, both)
        a_im[rows, :] = jnp.where(packed, even_minus, both)
        b_all[rows, :] = jnp.where(packed, 0.0, odd)
        return carry

    def prepare(chunk):
        @pl.when(low_side)
        def _():
            k_to_neg[chunk].wait_recv()
            fold(neg, nd, nr, part_rows, SLOTS - (chunk + 1) * part_rows)

        @pl.when(jnp.logical_not(low_side))
        def _():
            k_to_pos[chunk].wait_recv()
            fold(pos, pd, pr, part_rows, chunk * part_rows)

        first = chunk * part_rows
        lax.fori_loop(first, first + part_rows, combine, 0, unroll=4)

    def dip(chunk, quad, carry):
        got = jnp.concatenate(
            [rcv[chunk, pl.ds(comp * QUADS + quad, COUNT, stride=ROWS), :] for comp in range(2)], 1
        )
        first = table_dot(tab["t3"][...], got)
        cos, sin = tab["tw3c"][...], tab["tw3s"][...]
        spec = []
        for comp in range(2):
            real = first[:256, comp * 128 : (comp + 1) * 128]
            imag = first[256:, comp * 128 : (comp + 1) * 128]
            turned = jnp.concatenate([real * cos + imag * sin, imag * cos - real * sin], 1)
            spec.append(table_dot_t(tab["t4"][...], turned))
        rows = pl.ds(pl.multiple_of((chunk * QUADS + quad) * 64, 64), 64)
        b = b_all[rows, :]
        cos, sin = tab["tw5c"][...], tab["tw5s"][...]
        turned = []
        for even, odd in (
            (spec[0] * a_re[rows, :], spec[1] * b),
            (spec[1] * a_im[rows, :], -spec[0] * b),
        ):
            out = table_dot(tab["t5"][...], jnp.concatenate([even, odd], 0))
            real, imag = out[:128], out[128:]
            turned.append(
                jnp.concatenate([real * cos - imag * sin, real * sin + imag * cos], 1)
            )
        out = table_dot_t(tab["t6"][...], jnp.concatenate(turned, 0))
        for comp in range(2):
            snd2[chunk, pl.ds(comp * QUADS + quad, COUNT, stride=ROWS), :] = out[
                :, comp * 128 : (comp + 1) * 128
            ]
        return carry

    backward = []
    for chunk in range(CHUNKS):
        prepare(chunk)
        own, rest = forward[chunk]
        own.wait()
        rest.wait_recv()
        lax.fori_loop(0, QUADS, functools.partial(dip, chunk), 0, unroll=QUADS)
        backward.append(exchange(snd2, rcv2, chunk, 3))

    def unstrike(chunk, side, quad, carry):
        start = side * 64 * ROWS + quad
        got = jnp.concatenate(
            [
                rcv2[chunk, pl.ds(start + comp * QUADS, 64, stride=ROWS), :]
                for comp in range(2)
            ],
            0,
        )
        high, low = split(got.T)
        out = dot(jnp.concatenate([high, low, high], 1), tab["t7b" if side else "t7a"][...])
        real, imag = out[:, :128], out[:, 128:]
        if side == 0 and chunk == 0:
            alt = tab["alt"][...]
            extra = dot(high[:, 64:], alt) + dot(low[:, 64:], alt)
            line = lax.broadcasted_iota(jnp.int32, (128, 128), 0)
            keep = jnp.logical_and(line < LINES, quad == 0)
            real = real + jnp.where(keep, extra, 0.0)
        for part in range(4):
            freq = side * 32 + (chunk * QUADS + quad) * 4 + part
            cos = tab["tw1c"][pl.ds(freq, 1), :]
            sin = tab["tw1s"][pl.ds(freq, 1), :]
            rows = pl.ds(pl.multiple_of(freq * LINES, LINES), LINES)
            r, i = real[part * 32 : part * 32 + 32], imag[part * 32 : part * 32 + 32]
            yr[rows, :] = r * cos - i * sin
            yi[rows, :] = r * sin + i * cos
        return carry

    for chunk in range(CHUNKS):
        own, rest = backward[chunk]
        own.wait()
        rest.wait_recv()
        for side in range(2):
            lax.fori_loop(
                0, QUADS, functools.partial(unstrike, chunk, side), 0, unroll=QUADS
            )

    def last(pair, carry):
        both = jnp.concatenate(
            [
                jnp.concatenate(
                    [
                        yr[pl.ds(2 * pair + i, 64, stride=LINES), :],
                        yi[pl.ds(2 * pair + i, 64, stride=LINES), :],
                    ],
                    0,
                )
                for i in range(2)
            ],
            1,
        )
        out = table_dot(tab["t8"][...], both)
        for i in range(2):
            ebuf[pl.ds(2 * pair + i, 64, stride=LINES), :] = out[:, i * 128 : (i + 1) * 128]
        return carry

    def relay_back(first, side, dst, dst_first, col, carry):
        rows = pl.ds(pl.multiple_of((side * 32 + col) * LINES + first, 8), 8)
        lanes = pl.ds(pl.multiple_of(col * 128, 128), 128)
        dst[pl.ds(pl.multiple_of(dst_first, 8), 8), lanes] = ebuf[rows, :]
        return carry

    outgoing = []
    for part in range(LINES // 8):
        first = part * 8
        lax.fori_loop(part * 4, part * 4 + 4, last, 0, unroll=4)
        away = functools.partial(relay_back, first, 1 - rep, xout, first)
        lax.fori_loop(0, 32, away, 0, unroll=8)
        copy = pltpu.make_async_remote_copy(
            src_ref=xout.at[pl.ds(first, 8)],
            dst_ref=elastic.at[pl.ds(pl.multiple_of(rep * LINES + first, 8), 8)],
            send_sem=out_sems.at[0, part],
            recv_sem=out_sems.at[1, part],
            device_id=near,
            device_id_type=MESH,
        )
        copy.start()
        outgoing.append(copy)
    for part in range(LINES // 8):
        home = functools.partial(
            relay_back, part * 8, rep, elastic, rep * LINES + part * 8
        )
        lax.fori_loop(0, 32, home, 0, unroll=8)

    slip_out.wait_send()
    for own, rest in forward + backward:
        rest.wait_send()

    @pl.when(low_side)
    def _():
        for copy in k_to_pos:
            copy.wait_send()

    @pl.when(jnp.logical_not(low_side))
    def _():
        for copy in k_to_neg:
            copy.wait_send()
        edge_out.wait_send()

    for copy in outgoing:
        copy.wait()


def elastic_stress(slip_field, kernel_spectrum):
    made = tables()
    arrays = [jnp.asarray(made[name]) for name in NAMES]
    vmem = pl.BlockSpec(memory_space=pltpu.VMEM)
    flat = (64 * LINES, 128)
    packets = (CHUNKS, COUNT * ROWS, 128)
    return pl.pallas_call(
        body,
        out_shape=jax.ShapeDtypeStruct((64, 4096), F32),
        in_specs=[pl.BlockSpec(memory_space=pl.ANY)] * (2 + len(arrays)),
        out_specs=vmem,
        scratch_shapes=[pltpu.VMEM(a.shape, a.dtype) for a in arrays]
        + [pltpu.SemaphoreType.DMA((len(arrays),))]
        + [
            pltpu.VMEM((2, LINES, 4096), F32),
            pltpu.VMEM(flat, F32),
            pltpu.VMEM(flat, F32),
            pltpu.VMEM(flat, F32),
            pltpu.VMEM(packets, F32),
            pltpu.VMEM(packets, F32),
            pltpu.VMEM((SLOTS, 8192), F32),
            pltpu.VMEM((SLOTS, 8192), F32),
            pltpu.VMEM((1, 8192), F32),
            pltpu.VMEM((2, 512, 128), F32),
            pltpu.VMEM((2, 512, 128), F32),
            pltpu.VMEM((2, 528, 128), F32),
            pltpu.VMEM((2, 528, 128), F32),
            pltpu.VMEM((512, 256), F32),
            pltpu.VMEM((512, 256), F32),
            pltpu.VMEM((512, 256), F32),
            pltpu.VMEM(packets, F32),
            pltpu.VMEM(packets, F32),
            pltpu.VMEM(flat, F32),
            pltpu.VMEM((LINES, 4096), F32),
            pltpu.SemaphoreType.DMA((9,)),
            pltpu.SemaphoreType.DMA((2, CHUNKS)),
            pltpu.SemaphoreType.DMA((6, CHUNKS)),
            pltpu.SemaphoreType.DMA((2, LINES // 8)),
        ],
        compiler_params=pltpu.CompilerParams(
            collective_id=1, has_side_effects=True, vmem_limit_bytes=60 * 2**20
        ),
        name="elastic_stress",
    )(slip_field, kernel_spectrum, *arrays)


def shards(slip_field, state_field, direct_effect, load_stress, kernel_spectrum):
    elastic = elastic_stress(slip_field, kernel_spectrum)
    stress = load_stress + elastic
    velocity = (
        2.0
        * jnp.sinh(stress / direct_effect)
        * jnp.exp(-state_exponent * jnp.log(state_field) / direct_effect)
    )
    state_next = (state_field + time_step) / (1.0 + time_step * jnp.abs(velocity))
    return (velocity, state_next)


def solution(mesh):
    placed = (
        P("dip", "rep"),
        P("dip", "rep"),
        P("dip", "rep"),
        P("dip", "rep"),
        P(("dip", "rep"), None),
    )
    return jax.shard_map(
        shards,
        mesh=mesh,
        in_specs=placed,
        out_specs=(P("dip", "rep"), P("dip", "rep")),
        check_vma=False,
    )
```
